1024 devices in a mesh: expert: 16 (over z), tensor: 64 (over y, x, core).
Axes of the slice: x: 4, y: 8, z: 16, core: 2. Of those that a mesh axis runs over, the one named last changes fastest.
Arguments:
- tokens: bfloat16 [192, 6144], P('expert', 'tensor'), may hold values from -6 to 6
- out_grad: bfloat16 [192, 6144], P('expert', 'tensor'), may hold values from -1.5 to 1.5
- expert_ids: int32 [192, 4], P('expert'), may hold values from 0 to 7, all different within a row; in each aligned block of 12 rows (0 to 11, 12 to 23, ...) at most 10 rows name the same one
- gate_probs: float32 [192, 4], P('expert'), may hold values from 0.05 to 1
- w_gate: bfloat16 [16, 5376, 6144], P('expert', 'tensor'), may hold values from -0.21875 to 0.21875
- w_up: bfloat16 [16, 5376, 6144], P('expert', 'tensor'), may hold values from -0.21875 to 0.21875
- w_down: bfloat16 [16, 5376, 6144], P('expert', 'tensor'), may hold values from -0.0625 to 0.0625
Outputs:
- token_grad: bfloat16 [192, 6144], P('expert', 'tensor')
- gate_grad: float32 [192, 4], P('expert')
The draws below stay inside these ranges and needn't reach their ends.
Inputs may be any that keep to these rules, and one draw needn't show every extreme that they name: `expert_ids`: each token names 4 different experts. In the rows of one device (aligned blocks of 12 tokens) no expert is named more than 10 times, a bound that some block reaches.
All inputs are finite; a program needn't handle non-finite values.
Results may differ from the reference program's by a relative error of at most 0.011.
Values may be sent and summed in bfloat16 or wider, within the bound.
A program may use at most 32 MiB of HBM per device.

```python
import math
import jax
import jax.numpy as jnp
import numpy as np
from jax import lax

D = 6144
FF = 10752
TOP = 4
TOK_DEV = 12
EXPERTS = 8
SPLIT = 2
SLOTS = 10
TOKENS = 192
N_EXPERT = 16


def raised(result, rng, source, target, parts, factor):
    def block_of(axis_at):
        return (jnp.arange(result.shape[axis_at]) // (result.shape[axis_at] // parts)).reshape((-1,) + (1,) * (result.ndim - 1 - axis_at))

    near = jax.random.permutation(rng, parts)[block_of(target)]
    far = (block_of(target) + parts // 2) % parts
    return jnp.where((block_of(source) == near) | (block_of(source) == far), factor * result, result)


def shard_levels(own_key, shape, split, low, largest):
    gain, own = 1.0, jax.random.fold_in(own_key, 6)
    for axis_at, blocks in split:
        heights = jnp.exp(jax.random.uniform(jax.random.fold_in(own, axis_at), (blocks,), jnp.float32, low / len(split), largest / len(split)))
        gain = gain * jnp.repeat(heights, shape[axis_at] // blocks).reshape([-1 if axis == axis_at else 1 for axis in range(len(shape))])
    return gain


def routed_block(stream_key, own, number, rows, amount, top, reach, lean):
    order = jax.random.permutation(stream_key, amount)
    packed, usual = portions_of(amount, rows * top, reach, lean, True), portions_of(amount, rows * top, reach, lean, False)
    places = jnp.arange(amount)

    def named(lengths, rotation):
        used = int((lengths > 0).sum())
        fixed = max(1, used // 4)
        shifted = fixed + (places - fixed + rotation * (used - fixed)) % max(1, amount - fixed)
        return jnp.zeros((amount,), jnp.int32).at[order[jnp.where(places < fixed, places, shifted)]].set(jnp.asarray(lengths, jnp.int32))

    lengths = jnp.where(number % 4 == 0, named(packed, number // 4), named(usual, number - number // 4 - 1))
    mixed = jax.random.permutation(jax.random.fold_in(own, 3), amount)
    donor, sink = mixed[0:amount // 2 * 2:2], mixed[1:amount // 2 * 2:2]
    slack = jnp.minimum(lengths[donor] - 1, reach - lengths[sink]) // 2
    slack = jnp.where((donor == order[0]) | (sink == order[0]) | (lengths[sink] == 0), 0, jnp.maximum(slack, 0))
    shifted = jax.random.randint(jax.random.fold_in(own, 4), (amount // 2,), 0, 1 << 20) % (slack + 1)
    lengths = lengths.at[donor].add(-shifted).at[sink].add(shifted)
    members = jnp.searchsorted(jnp.cumsum(lengths), jnp.arange(rows * top), side="right").astype(jnp.int32)
    listing = members.reshape(top, rows).T
    listing = listing[jax.random.permutation(jax.random.fold_in(own, 1), rows)]
    rotation = jax.random.randint(jax.random.fold_in(own, 2), (rows, 1), 0, top)
    return jnp.take_along_axis(listing, (jnp.arange(top)[None, :] + rotation) % top, axis=1)


def portions_of(number_of, total, most, lean, full):
    loads = [(1 << 20) // math.isqrt(standing ** lean) + 1 for standing in range(1, number_of + 1)]
    largest = most if full else min(most, max(-(-total // number_of), total * loads[0] // sum(loads)))
    least = 1 if total - largest >= number_of - 1 else 0
    holding, rest = [largest] + [least] * (number_of - 1), total - largest - least * (number_of - 1)
    while rest > 0:
        movable = [i for i in range(1, number_of) if holding[i] < largest] or [i for i in range(1, number_of) if holding[i] < most]
        mass, remaining = sum([loads[i] for i in movable]), rest
        for i in movable:
            extra = min(most - holding[i], max(1, remaining * loads[i] // mass), rest)
            holding[i] = holding[i] + extra
            rest = rest - extra
    return np.array(holding)


def bell_draw(key, extent, scale, limit, split=(), kind=jnp.bfloat16):
    result = jax.random.normal(key, extent, jnp.float32) * scale
    if len(split) > 0:
        result = shard_levels(key, extent, split, -0.22, 0.18) * result
    return jnp.clip(result, min=-limit, max=limit).astype(kind)


def bell_draw_with(rng, dims, width, limit, pieces, heavy, kind=jnp.bfloat16):
    values = width * jax.random.normal(rng, dims, jnp.float32)
    if pieces:
        values = values * shard_levels(rng, dims, pieces, -0.22, 0.18)
    return jnp.clip(raised(values, jax.random.fold_in(rng, 3), *heavy), -limit, limit).astype(kind)


def setup_inputs(seed: int = 0) -> dict:
    key_of = jax.random.split(jax.random.key(seed), 8)
    tokens = bell_draw(key_of[0], (TOKENS, D), 1.0, 6.0, ((0, 16), (1, 64)))
    out_grad = bell_draw(key_of[1], (TOKENS, D), 0.2, 1.5, ((0, 16), (1, 64)))
    expert_ids_keys = jax.random.split(jax.random.fold_in(key_of[2], 1), TOKENS // TOK_DEV)
    expert_ids_turns = jax.random.permutation(jax.random.fold_in(key_of[2], 3), TOKENS // TOK_DEV)
    expert_ids = jax.vmap(lambda own, number: routed_block(jax.random.fold_in(key_of[2], 2), own, number, TOK_DEV, EXPERTS, TOP, SLOTS, 2))(expert_ids_keys, expert_ids_turns).reshape((TOKENS, TOP))
    gate_probs = jnp.clip(jnp.exp(math.log(1.0) - 2.9957323 * jax.random.uniform(key_of[3], (TOKENS, TOP), jnp.float32) ** shard_levels(key_of[3], (TOKENS, TOP), ((0, 16),), -0.2, 0.2)), 0.05, 1.0)
    w_gate = bell_draw_with(key_of[4], (N_EXPERT, FF // SPLIT, D), D ** -0.5, 0.21875, ((0, 16), (1, 64)), (1, 2, 64, 4.0))
    w_up = bell_draw_with(key_of[5], (N_EXPERT, FF // SPLIT, D), D ** -0.5, 0.21875, ((0, 16), (1, 64)), (1, 2, 64, 4.0))
    w_down = bell_draw(key_of[6], (N_EXPERT, FF // SPLIT, D), FF ** -0.5, 0.0625, ((0, 16), (1, 64)))
    return dict(tokens=tokens, out_grad=out_grad, expert_ids=expert_ids, gate_probs=gate_probs, w_gate=w_gate, w_up=w_up, w_down=w_down)


def reference(tokens, out_grad, expert_ids, gate_probs, w_gate, w_up, w_down):
    n_halves = w_gate.shape[0]
    half_count = n_halves // EXPERTS
    chosen = expert_ids[:, :, None] == jnp.arange(EXPERTS, dtype=jnp.int32)[None, None, :]
    expert_weight = jnp.sum(jnp.where(chosen, gate_probs[:, :, None], jnp.float32(0.0)), axis=1)

    def advance(running, inputs):
        grad_total, gate_total = running
        gate_piece, up_piece, down_piece, half_index = inputs
        expert = half_index // half_count
        pre_gate = lax.dot_general(tokens, gate_piece, (((1,), (1,)), ((), ())), preferred_element_type=jnp.float32)
        pre_up = lax.dot_general(tokens, up_piece, (((1,), (1,)), ((), ())), preferred_element_type=jnp.float32)
        back = lax.dot_general(out_grad, down_piece, (((1,), (1,)), ((), ())), preferred_element_type=jnp.float32)
        sigmoid_val = jax.nn.sigmoid(pre_gate)
        activated = pre_gate * sigmoid_val
        slope_term = sigmoid_val * (1.0 + pre_gate * (1.0 - sigmoid_val))
        hidden = (activated * pre_up).astype(jnp.bfloat16)
        gate_terms = jnp.sum(hidden.astype(jnp.float32) * back, axis=1)
        grad_gate = (back * pre_up * slope_term).astype(jnp.bfloat16)
        grad_up = (back * activated).astype(jnp.bfloat16)
        partial_grad = jnp.dot(grad_gate, gate_piece, preferred_element_type=jnp.float32)
        partial_grad = partial_grad + jnp.dot(grad_up, up_piece, preferred_element_type=jnp.float32)
        column = (jnp.arange(EXPERTS, dtype=jnp.int32) == expert).astype(jnp.float32)
        gate_scale = jnp.sum(expert_weight * column[None, :], axis=1)
        grad_total = grad_total + gate_scale[:, None] * partial_grad
        gate_total = gate_total + gate_terms[:, None] * column[None, :]
        return (grad_total, gate_total), None

    initial = (jnp.zeros((TOKENS, D), jnp.float32), jnp.zeros((TOKENS, EXPERTS), jnp.float32))
    (grad_total, gate_total), _ = lax.scan(advance, initial, (w_gate, w_up, w_down, jnp.arange(n_halves, dtype=jnp.int32)))
    gate_grad = jnp.sum(jnp.where(chosen, gate_total[:, None, :], jnp.float32(0.0)), axis=2)
    return grad_total.astype(jnp.bfloat16), gate_grad
```

```python
import jax
import jax.numpy as jnp
from jax import lax
from jax.experimental import pallas as pl
from jax.experimental.pallas import tpu as pltpu
from jax.sharding import PartitionSpec as P

MESH = pl.DeviceIdType.MESH
BF = jnp.bfloat16
F32 = jnp.float32
NZ, NY, NX = 16, 8, 4
SLICES = NY * NX
HID = 84
HPAD = 96
FEAT = 96
LANE = 128
TOK = 12
ROWS = NZ * TOK
COLS = 2 * ROWS
WIDE = NY * LANE


def iota(shape, dim):
    return lax.broadcasted_iota(jnp.int32, shape, dim)


def dot(a, b, ca=1, cb=0):
    return lax.dot_general(a, b, (((ca,), (cb,)), ((), ())), preferred_element_type=F32)


def kernel(
    tok, grad, ids, probs, wg, wu, wd,
    tg_out, gg_out,
    wraw, wr, wall, zsend, zbuf, xbuf, part, part2, gcat,
    xs, xr, ysend, yrecv, rsend, rrecv,
    wsem, lsem, ssem, csem,
    zss, zrs, xss, xrs, yss, yrs, rxs, rxr, rys, ryr, rzs, rzr,
):
    z = lax.axis_index("expert")
    t = lax.axis_index("tensor")
    y = t // 8
    x = lax.rem(t // 2, 4)
    c = lax.rem(t, 2)
    other = 1 - c

    def dev(zz, yy, xx, cc):
        return (zz, (yy * NX + xx) * 2 + cc)

    def zdev(d):
        return dev(lax.rem(z + d, NZ), y, x, c)

    def ydev(d):
        return dev(z, lax.rem(y + d, NY), x, c)

    def xdev(d):
        return dev(z, y, lax.rem(x + d, NX), c)

    sibling = dev(z, y, x, other)

    def remote(src, dst, ss, rs, target):
        return pltpu.make_async_remote_copy(
            src_ref=src, dst_ref=dst, send_sem=ss, recv_sem=rs, device_id=target, device_id_type=MESH
        )

    bar = pltpu.get_barrier_semaphore()

    def greet_z(d, carry):
        pl.semaphore_signal(bar, inc=1, device_id=zdev(d), device_id_type=MESH)
        return carry

    def greet_y(d, carry):
        pl.semaphore_signal(bar, inc=1, device_id=ydev(d), device_id_type=MESH)
        return carry

    def greet_x(d, carry):
        pl.semaphore_signal(bar, inc=1, device_id=xdev(d), device_id_type=MESH)
        return carry

    lax.fori_loop(1, NZ, greet_z, 0)
    lax.fori_loop(1, NY, greet_y, 0)
    lax.fori_loop(1, NX, greet_x, 0)
    pl.semaphore_signal(bar, inc=1, device_id=sibling, device_id_type=MESH)

    loads = [
        pltpu.make_async_copy(src.at[0], wraw.at[i], wsem.at[i]) for i, src in enumerate((wg, wu, wd))
    ]
    for cp in loads:
        cp.start()

    zsend[...] = jnp.zeros_like(zsend)
    zsend[0:TOK, 0:FEAT] = tok[...]
    zsend[16:16 + TOK, 0:FEAT] = grad[...]
    zbuf[z] = zsend[...]

    pl.semaphore_wait(bar, (NZ - 1) + (NY - 1) + (NX - 1) + 1)

    def zcopy(d):
        return remote(zsend, zbuf.at[z], zss.at[d], zrs.at[d], zdev(d))

    def zstart(i, carry):
        zcopy(lax.rem(i + 7, 15) + 1).start()
        return carry

    lax.fori_loop(0, NZ - 1, zstart, 0)

    xbuf[:, FEAT:LANE, :] = jnp.zeros((SLICES, LANE - FEAT, COLS), BF)
    wr[:, :, 80:HPAD, :] = jnp.zeros((2, 3, HPAD - 80, SLICES * LANE), BF)
    row = iota((4 * FEAT, 4 * LANE), 0)
    q = (
        (row >= FEAT).astype(jnp.int32)
        + (row >= 2 * FEAT).astype(jnp.int32)
        + (row >= 3 * FEAT).astype(jnp.int32)
    )
    spread = jnp.where(iota((4 * FEAT, 4 * LANE), 1) == row + q * (LANE - FEAT), 1.0, 0.0).astype(BF)
    for cp in loads:
        cp.wait()

    def relay(g, carry):
        yy = g // 2
        xx = 2 * lax.rem(g, 2)
        for i in range(3):
            wide = dot(
                wraw[i, :, pl.ds(pl.multiple_of(g * (4 * FEAT), LANE), 4 * FEAT)], spread
            ).astype(BF)
            for j in range(4):
                at = pl.multiple_of(((xx + j // 2) * NY + yy) * LANE, LANE)
                wr[j % 2, i, 0:HID, pl.ds(at, LANE)] = wide[:, j * LANE:(j + 1) * LANE]
        return carry

    lax.fori_loop(0, 16, relay, 0)
    wsend = remote(wr.at[other], wall.at[:, c], ssem.at[0], ssem.at[1], sibling)
    wsend.start()
    wown = pltpu.make_async_copy(wr.at[c], wall.at[:, c], lsem.at[0])
    wown.start()

    def zwait(d, carry):
        zcopy(d).wait_recv()
        return carry

    lax.fori_loop(1, NZ, zwait, 0)
    r = iota((NZ * 32, COLS), 0)
    col = iota((NZ * 32, COLS), 1)
    want = ((r >> 4) & 1) * ROWS + (r >> 5) * TOK + (r & 15)
    pick = jnp.where((col == want) & ((r & 15) < TOK), 1.0, 0.0).astype(BF)
    mine = dot(zbuf[...].reshape(NZ * 32, LANE), pick, 0, 0).astype(BF)
    slot = x * NY + y
    xbuf[slot, 0:FEAT, :] = mine[0:FEAT, :]

    def xcopy(d):
        return remote(
            xbuf.at[slot, pl.ds(0, FEAT)], xbuf.at[slot, pl.ds(0, FEAT)], xss.at[d], xrs.at[d], xdev(d)
        )

    for d in (2, 1, 3):
        xcopy(d).start()

    half = FEAT // 2

    def ycopy(i, s, way):
        xx = lax.rem(x + NX - i, NX)
        yy = lax.rem(y + NY - s, NY) if way == 0 else lax.rem(y + s, NY)
        rows = pl.ds(0, FEAT) if s < 3 else pl.ds(way * half, half)
        ref = xbuf.at[xx * NY + yy, rows]
        return remote(ref, ref, yss.at[way, i, s], yrs.at[way, i, s], ydev(1 if way == 0 else NY - 1))

    for i in (0, 1, 3, 2):
        if i:
            xcopy(i).wait_recv()
        ycopy(i, 0, 0).start()
        ycopy(i, 0, 1).start()
    for s in (1, 2, 3):
        for i in (0, 1, 3, 2):
            for way in (0, 1):
                ycopy(i, s - 1, way).wait_recv()
                ycopy(i, s, way).start()
    for i in (0, 1, 3, 2):
        for way in (0, 1):
            ycopy(i, 3, way).wait_recv()

    wown.wait()
    wsend.wait_recv()
    part[...] = jnp.zeros_like(part)

    def forward(k, carry):
        lanes = pl.ds(pl.multiple_of(k * WIDE, LANE), WIDE)
        blk = xbuf[pl.ds(k * NY, NY)].reshape(WIDE, COLS)
        both = wall[0:2, :, :, lanes].reshape(4 * HPAD, WIDE)
        part[0:2] += dot(both, blk[:, 0:256]).reshape(2, 2 * HPAD, 256)
        part[2] += dot(wall[2, :, :, lanes].reshape(2 * HPAD, WIDE), blk[:, 128:384])
        return carry

    lax.fori_loop(0, NX, forward, 0)
    psend = remote(part, part2, csem.at[0], csem.at[1], sibling)
    psend.start()
    psend.wait()
    pre_gate = (part[0] + part2[0])[:, 0:ROWS]
    pre_up = (part[1] + part2[1])[:, 0:ROWS]
    back = (part[2] + part2[2])[:, 64:64 + ROWS]
    sig = jax.nn.sigmoid(pre_gate)
    act = pre_gate * sig
    slope = sig * (1.0 + pre_gate * (1.0 - sig))
    hidden = (act * pre_up).astype(BF).astype(F32)
    terms = jnp.sum(hidden * back, axis=0, keepdims=True)
    gcat[0:2 * HPAD, :] = (back * pre_up * slope).astype(BF)
    gcat[2 * HPAD:4 * HPAD, :] = (back * act).astype(BF)

    def gate_lanes(column, rows):
        hi = column.astype(BF).astype(F32)
        lane = iota((rows, LANE), 1)
        return jnp.where(lane == FEAT, hi, jnp.where(lane == FEAT + 1, column - hi, 0.0))

    eye = iota((ROWS, ROWS), 0) == iota((ROWS, ROWS), 1)
    column = jnp.sum(jnp.where(eye, terms, 0.0), axis=1, keepdims=True)
    ride = gate_lanes(column, ROWS)
    ride = jnp.concatenate([ride] * NY, axis=1)

    gt = gcat[...]

    def block(xx):
        lanes = pl.ds(pl.multiple_of(xx * WIDE, LANE), WIDE)
        return dot(gt, wall[0:2, :, :, lanes].reshape(4 * HPAD, WIDE), 0, 0) + ride

    def rxcopy(d):
        return remote(xs.at[d - 1], xr.at[d - 1], rxs.at[d], rxr.at[d], xdev(d))

    for d in (2, 1, 3):
        xs[d - 1] = block(lax.rem(x + d, NX)).astype(BF)
        rxcopy(d).start()
    total = block(x)
    for d in (1, 3, 2):
        rxcopy(d).wait_recv()
        total = total + xr[d - 1].astype(F32)

    def regate(v, rows):
        lane = iota((rows, LANE), 1)
        gate = jnp.sum(
            jnp.where((lane == FEAT) | (lane == FEAT + 1), v, 0.0), axis=1, keepdims=True
        )
        return gate_lanes(gate, rows), lane < FEAT

    ride, body = regate(total[:, 0:LANE], ROWS)
    for i in range(NY):
        ysend[i] = jnp.where(body, total[:, i * LANE:(i + 1) * LANE], ride).astype(BF)

    def rycopy(d):
        return remote(ysend.at[lax.rem(y + d, NY)], yrecv.at[d], rys.at[d], ryr.at[d], ydev(d))

    for d in (4, 3, 5, 2, 6, 1, 7):
        rycopy(d).start()
    acc = ysend[y].astype(F32)
    for d in (1, 7, 2, 6, 3, 5, 4):
        rycopy(d).wait_recv()
        acc = acc + yrecv[d].astype(F32)

    ride, body = regate(acc, ROWS)
    acc = jnp.where(body, acc, ride).astype(BF)
    r = iota((NZ * 16, ROWS), 0)
    place = (iota((NZ * 16, ROWS), 1) == (r >> 4) * TOK + (r & 15)) & ((r & 15) < TOK)
    rsend[...] = dot(jnp.where(place, 1.0, 0.0).astype(BF), acc).astype(BF).reshape(NZ, 16, LANE)
    rrecv[z] = rsend[z]

    def rzcopy(d):
        return remote(rsend.at[lax.rem(z + d, NZ)], rrecv.at[z], rzs.at[d], rzr.at[d], zdev(d))

    def rzstart(i, carry):
        rzcopy(lax.rem(i + 7, 15) + 1).start()
        return carry

    lax.fori_loop(0, NZ - 1, rzstart, 0)

    def rzwait(d, carry):
        rzcopy(d).wait_recv()
        return carry

    lax.fori_loop(1, NZ, rzwait, 0)
    chosen = ids[...]
    weight = probs[...]
    out = jnp.zeros((TOK, LANE), F32)
    gout = jnp.zeros((TOK, 4), F32)
    for e in range(NZ // 2):
        hit = chosen == e
        w = jnp.sum(jnp.where(hit, weight, 0.0), axis=1, keepdims=True)
        v = rrecv[2 * e].astype(F32) + rrecv[2 * e + 1].astype(F32)
        v = v[0:TOK]
        out = out + w * v
        gate = v[:, FEAT:FEAT + 1] + v[:, FEAT + 1:FEAT + 2]
        gout = gout + jnp.where(hit, gate, 0.0)
    tg_out[...] = out[:, 0:FEAT].astype(BF)
    gg_out[...] = gout

    def zdone(d, carry):
        zcopy(d).wait_send()
        rzcopy(d).wait_send()
        return carry

    lax.fori_loop(1, NZ, zdone, 0)
    wsend.wait_send()
    for d in range(1, NX):
        xcopy(d).wait_send()
        rxcopy(d).wait_send()
    for d in range(1, NY):
        rycopy(d).wait_send()
    for s in range(4):
        for i in range(NX):
            for way in (0, 1):
                ycopy(i, s, way).wait_send()


def body(tokens, out_grad, expert_ids, gate_probs, w_gate, w_up, w_down):
    vmem = pl.BlockSpec(memory_space=pltpu.VMEM)
    hbm = pl.BlockSpec(memory_space=pl.ANY)
    dma = pltpu.SemaphoreType.DMA
    return pl.pallas_call(
        kernel,
        out_shape=(
            jax.ShapeDtypeStruct((TOK, FEAT), BF),
            jax.ShapeDtypeStruct((TOK, 4), F32),
        ),
        in_specs=[vmem, vmem, vmem, vmem, hbm, hbm, hbm],
        out_specs=(vmem, vmem),
        scratch_shapes=[
            pltpu.VMEM((3, HID, SLICES * 2 * FEAT), BF),
            pltpu.VMEM((2, 3, HPAD, SLICES * LANE), BF),
            pltpu.VMEM((3, 2, HPAD, SLICES * LANE), BF),
            pltpu.VMEM((32, LANE), BF),
            pltpu.VMEM((NZ, 32, LANE), BF),
            pltpu.VMEM((SLICES, LANE, COLS), BF),
            pltpu.VMEM((3, 2 * HPAD, 256), F32),
            pltpu.VMEM((3, 2 * HPAD, 256), F32),
            pltpu.VMEM((4 * HPAD, ROWS), BF),
            pltpu.VMEM((NX - 1, ROWS, WIDE), BF),
            pltpu.VMEM((NX - 1, ROWS, WIDE), BF),
            pltpu.VMEM((NY, ROWS, LANE), BF),
            pltpu.VMEM((NY, ROWS, LANE), BF),
            pltpu.VMEM((NZ, 16, LANE), BF),
            pltpu.VMEM((NZ, 16, LANE), BF),
            dma((3,)),
            dma((1,)),
            dma((2,)),
            dma((2,)),
            dma((NZ,)), dma((NZ,)),
            dma((NX,)), dma((NX,)),
            dma((2, NX, 4)), dma((2, NX, 4)),
            dma((NX,)), dma((NX,)),
            dma((NY,)), dma((NY,)),
            dma((NZ,)), dma((NZ,)),
        ],
        compiler_params=pltpu.CompilerParams(
            collective_id=0, has_side_effects=True, vmem_limit_bytes=48 * 2**20
        ),
    )(tokens, out_grad, expert_ids, gate_probs, w_gate, w_up, w_down)


def solution(mesh):
    in_specs = (
        P("expert", "tensor"),
        P("expert", "tensor"),
        P("expert", None),
        P("expert", None),
        P("expert", "tensor", None),
        P("expert", "tensor", None),
        P("expert", "tensor", None),
    )
    out_specs = (P("expert", "tensor"), P("expert", None))
    return jax.shard_map(body, mesh=mesh, in_specs=in_specs, out_specs=out_specs, check_vma=False)
```

```python
import jax
import jax.numpy as jnp
from jax import lax
from jax.experimental import pallas as pl
from jax.experimental.pallas import tpu as pltpu
from jax.sharding import PartitionSpec as P

MESH = pl.DeviceIdType.MESH
BF = jnp.bfloat16
F32 = jnp.float32
NZ, NY, NX = 16, 8, 4
SLICES = NY * NX
HID = 84
HPAD = 96
FEAT = 96
LANE = 128
TOK = 12
ROWS = NZ * TOK
COLS = 2 * ROWS
WIDE = NY * LANE


def iota(shape, dim):
    return lax.broadcasted_iota(jnp.int32, shape, dim)


def dot(a, b, ca=1, cb=0):
    return lax.dot_general(a, b, (((ca,), (cb,)), ((), ())), preferred_element_type=F32)


def kernel(
    tok, grad, ids_in, probs_in, wg, wu, wd,
    tg_out, gg_out,
    tin, ids, probs, wraw, wr, wall, zsend, zbuf, xbuf, part, part2, gcat, tmine, tother,
    xs1, xr1, xs2, xr2, ysend, yrecv, rsend, rrecv,
    tsem, wsem, lsem, ssem, csem,
    zss, zrs, xss, xrs, yss, yrs, s1s, s1r, s2s, s2r, rys, ryr, rzs, rzr,
):
    z = lax.axis_index("expert")
    t = lax.axis_index("tensor")
    y = t // 8
    x = lax.rem(t // 2, 4)
    c = lax.rem(t, 2)
    other = 1 - c

    def dev(zz, yy, xx, cc):
        return (zz, (yy * NX + xx) * 2 + cc)

    def zdev(d):
        return dev(lax.rem(z + d, NZ), y, x, c)

    def ydev(d):
        return dev(z, lax.rem(y + d, NY), x, c)

    def xdev(d):
        return dev(z, y, lax.rem(x + d, NX), c)

    sibling = dev(z, y, x, other)

    def remote(src, dst, ss, rs, target):
        return pltpu.make_async_remote_copy(
            src_ref=src, dst_ref=dst, send_sem=ss, recv_sem=rs, device_id=target, device_id_type=MESH
        )

    bar = pltpu.get_barrier_semaphore()

    def greet_z(d, carry):
        pl.semaphore_signal(bar, inc=1, device_id=zdev(d), device_id_type=MESH)
        return carry

    def greet_y(d, carry):
        pl.semaphore_signal(bar, inc=1, device_id=ydev(d), device_id_type=MESH)
        return carry

    def greet_x(d, carry):
        pl.semaphore_signal(bar, inc=1, device_id=xdev(d), device_id_type=MESH)
        return carry

    lax.fori_loop(1, NZ, greet_z, 0)
    lax.fori_loop(1, NY, greet_y, 0)
    lax.fori_loop(1, NX, greet_x, 0)
    pl.semaphore_signal(bar, inc=1, device_id=sibling, device_id_type=MESH)

    heads = [pltpu.make_async_copy(src, tin.at[i], tsem.at[i]) for i, src in enumerate((tok, grad))]
    heads.append(pltpu.make_async_copy(ids_in, ids, tsem.at[2]))
    heads.append(pltpu.make_async_copy(probs_in, probs, tsem.at[3]))
    for cp in heads:
        cp.start()
    loads = [
        pltpu.make_async_copy(src.at[0], wraw.at[i], wsem.at[i]) for i, src in enumerate((wg, wu, wd))
    ]
    for cp in loads:
        cp.start()

    zsend[...] = jnp.zeros_like(zsend)
    for cp in heads:
        cp.wait()
    zsend[0:TOK, 0:FEAT] = tin[0]
    zsend[16:16 + TOK, 0:FEAT] = tin[1]
    zbuf[z] = zsend[...]

    pl.semaphore_wait(bar, (NZ - 1) + (NY - 1) + (NX - 1) + 1)

    def zcopy(d):
        return remote(zsend, zbuf.at[z], zss.at[d], zrs.at[d], zdev(d))

    def zstart(i, carry):
        zcopy(lax.rem(i + 7, 15) + 1).start()
        return carry

    lax.fori_loop(0, NZ - 1, zstart, 0)

    xbuf[:, FEAT:LANE, :] = jnp.zeros((SLICES, LANE - FEAT, COLS), BF)
    wr[:, :, 80:HPAD, :] = jnp.zeros((2, 3, HPAD - 80, SLICES * LANE), BF)
    row = iota((4 * FEAT, 4 * LANE), 0)
    q = (
        (row >= FEAT).astype(jnp.int32)
        + (row >= 2 * FEAT).astype(jnp.int32)
        + (row >= 3 * FEAT).astype(jnp.int32)
    )
    spread = jnp.where(iota((4 * FEAT, 4 * LANE), 1) == row + q * (LANE - FEAT), 1.0, 0.0).astype(BF)
    for cp in loads:
        cp.wait()

    def relay(g, carry):
        yy = g // 2
        xx = 2 * lax.rem(g, 2)
        for i in range(3):
            wide = dot(
                wraw[i, :, pl.ds(pl.multiple_of(g * (4 * FEAT), LANE), 4 * FEAT)], spread
            ).astype(BF)
            for j in range(4):
                at = pl.multiple_of(((xx + j // 2) * NY + yy) * LANE, LANE)
                wr[j % 2, i, 0:HID, pl.ds(at, LANE)] = wide[:, j * LANE:(j + 1) * LANE]
        return carry

    lax.fori_loop(0, 16, relay, 0)
    wsend = remote(wr.at[other], wall.at[:, c], ssem.at[0], ssem.at[1], sibling)
    wsend.start()
    wown = pltpu.make_async_copy(wr.at[c], wall.at[:, c], lsem.at[0])
    wown.start()

    small = iota((TOK, TOK), 0) == iota((TOK, TOK), 1)

    def upright(ref, k, zero):
        return jnp.sum(jnp.where(small, ref[k:k + 1, :], zero), axis=1, keepdims=True)

    chosen = [upright(ids, k, 0) for k in range(4)]
    weight = [upright(probs, k, 0.0) for k in range(4)]

    def zwait(d, carry):
        zcopy(d).wait_recv()
        return carry

    lax.fori_loop(1, NZ, zwait, 0)
    r = iota((NZ * 32, COLS), 0)
    col = iota((NZ * 32, COLS), 1)
    want = ((r >> 4) & 1) * ROWS + (r >> 5) * TOK + (r & 15)
    pick = jnp.where((col == want) & ((r & 15) < TOK), 1.0, 0.0).astype(BF)
    mine = dot(zbuf[...].reshape(NZ * 32, LANE), pick, 0, 0).astype(BF)
    slot = x * NY + y
    xbuf[slot, 0:FEAT, :] = mine[0:FEAT, :]

    def xcopy(d):
        return remote(
            xbuf.at[slot, pl.ds(0, FEAT)], xbuf.at[slot, pl.ds(0, FEAT)], xss.at[d], xrs.at[d], xdev(d)
        )

    for d in (2, 1, 3):
        xcopy(d).start()

    half = FEAT // 2

    def ycopy(i, s, way):
        xx = lax.rem(x + NX - i, NX)
        yy = lax.rem(y + NY - s, NY) if way == 0 else lax.rem(y + s, NY)
        rows = pl.ds(0, FEAT) if s < 3 else pl.ds(way * half, half)
        ref = xbuf.at[xx * NY + yy, rows]
        return remote(ref, ref, yss.at[way, i, s], yrs.at[way, i, s], ydev(1 if way == 0 else NY - 1))

    def forward(i, cores):
        xx = lax.rem(x + NX - i, NX)
        lanes = pl.ds(pl.multiple_of(xx * WIDE, LANE), WIDE)
        blk = xbuf[pl.ds(xx * NY, NY)].reshape(WIDE, COLS)
        for cc in cores:
            pair = wall[0:2, cc, :, lanes].reshape(2 * HPAD, WIDE)
            pair = dot(pair, blk[:, 0:256]).reshape(2, HPAD, 256)
            down = dot(wall[2, cc, :, lanes], blk[:, 128:384])
            if i == 0:
                part[0:2, cc] = pair
                part[2, cc] = down
            else:
                part[0:2, cc] += pair
                part[2, cc] += down

    order = (
        (0, 0), (1, 0), (3, 0), (0, 1), (2, 0), (1, 1), (3, 1), (0, 2),
        (2, 1), (1, 2), (3, 2), (0, 3), (2, 2), (1, 3), (3, 3), (2, 3),
    )
    for i, s in order:
        if s == 0 and i:
            xcopy(i).wait_recv()
        for way in (0, 1):
            if s:
                ycopy(i, s - 1, way).wait_recv()
            ycopy(i, s, way).start()

    wown.wait()
    wsend.wait_recv()
    for i in (0, 1, 3, 2):
        for way in (0, 1):
            ycopy(i, 3, way).wait_recv()
        if i != 2:
            forward(i, (0, 1))
    forward(2, (other,))
    psend = remote(part.at[:, other], part2, csem.at[0], csem.at[1], sibling)
    psend.start()
    forward(2, (c,))
    psend.wait_recv()
    pre_gate = (part[0, c] + part2[0])[:, 0:ROWS]
    pre_up = (part[1, c] + part2[1])[:, 0:ROWS]
    back = (part[2, c] + part2[2])[:, 64:64 + ROWS]
    sig = jax.nn.sigmoid(pre_gate)
    act = pre_gate * sig
    slope = sig * (1.0 + pre_gate * (1.0 - sig))
    hidden = (act * pre_up).astype(BF).astype(F32)
    terms = jnp.sum(hidden * back, axis=0, keepdims=True)
    tmine[:, 0:ROWS] = jnp.broadcast_to(terms, (8, ROWS))
    gcat[0, c, :, 0:ROWS] = (back * pre_up * slope).astype(BF)
    gcat[1, c, :, 0:ROWS] = (back * act).astype(BF)
    tswap = remote(tmine, tother, csem.at[2], csem.at[3], sibling)
    tswap.start()
    gswap = remote(gcat.at[:, c], gcat.at[:, c], csem.at[4], csem.at[5], sibling)
    gswap.start()

    def gate_lanes(column, rows):
        hi = column.astype(BF).astype(F32)
        lane = iota((rows, LANE), 1)
        return jnp.where(lane == FEAT, hi, jnp.where(lane == FEAT + 1, column - hi, 0.0))

    def regate(v, rows):
        lane = iota((rows, LANE), 1)
        gate = jnp.sum(
            jnp.where((lane == FEAT) | (lane == FEAT + 1), v, 0.0), axis=1, keepdims=True
        )
        return gate_lanes(gate, rows), lane < FEAT

    def rewide(v, rows):
        ride, body = regate(v[:, 0:LANE], rows)
        return jnp.where(
            jnp.concatenate([body] * NY, axis=1), v, jnp.concatenate([ride] * NY, axis=1)
        ).astype(BF)

    eye = iota((ROWS, ROWS), 0) == iota((ROWS, ROWS), 1)
    tswap.wait_recv()
    terms = terms + tother[0:1, 0:ROWS]
    column = jnp.sum(jnp.where(eye, terms, 0.0), axis=1, keepdims=True)
    ride = jnp.concatenate([gate_lanes(column, ROWS)] * NY, axis=1)
    gswap.wait_recv()
    gt = gcat[...].reshape(4 * HPAD, 256)[:, 0:ROWS]

    def block(xx):
        lanes = pl.ds(pl.multiple_of(xx * WIDE, LANE), WIDE)
        return dot(gt, wall[0:2, :, :, lanes].reshape(4 * HPAD, WIDE), 0, 0) + ride

    nextx = (xdev(1), xdev(NX - 1))
    part_rows = ROWS // 2
    quarter = part_rows // 2

    def s1copy(h, way):
        return remote(xs1.at[h, way], xr1.at[h, way], s1s.at[h, way], s1r.at[h, way], nextx[way])

    def s2copy(h, way):
        return remote(xs2.at[h, way], xr2.at[h, way], s2s.at[h, way], s2r.at[h, way], nextx[way])

    far = block(lax.rem(x + 2, NX)).astype(BF)
    for h in (0, 1):
        for way in (0, 1):
            at = h * part_rows + way * quarter
            xs1[h, way] = far[at:at + quarter]
            s1copy(h, way).start()
    near = (block(lax.rem(x + 1, NX)), block(lax.rem(x + NX - 1, NX)))
    for h in (0, 1):
        for way in (0, 1):
            for w in (0, 1):
                at = h * part_rows + w * quarter
                mine = near[way][at:at + quarter]
                if w == way:
                    s1copy(h, way).wait_recv()
                    mine = rewide(mine + xr1[h, way].astype(F32), quarter)
                xs2[h, way, w * quarter:(w + 1) * quarter, :] = mine.astype(BF)
            s2copy(h, way).start()
    total = block(x)

    def rycopy(h, d):
        return remote(
            ysend.at[h, lax.rem(y + d, NY)], yrecv.at[h, d], rys.at[h, d], ryr.at[h, d], ydev(d)
        )

    for h in (0, 1):
        v = total[h * part_rows:(h + 1) * part_rows]
        for way in (0, 1):
            s2copy(h, way).wait_recv()
            v = v + xr2[h, way].astype(F32)
        v = rewide(v, part_rows)
        for i in range(NY):
            ysend[h, i] = v[:, i * LANE:(i + 1) * LANE]
        for d in (4, 3, 5, 2, 6, 1, 7):
            rycopy(h, d).start()

    blocks = NZ // 2
    r = iota((blocks * 16, part_rows), 0)
    place = (iota((blocks * 16, part_rows), 1) == (r >> 4) * TOK + (r & 15)) & ((r & 15) < TOK)
    place = jnp.where(place, 1.0, 0.0).astype(BF)

    def rzcopy(d):
        return remote(rsend.at[lax.rem(z + d, NZ)], rrecv.at[z], rzs.at[d], rzr.at[d], zdev(d))

    for h in (0, 1):
        acc = ysend[h, y].astype(F32)
        for d in (1, 7, 2, 6, 3, 5, 4):
            rycopy(h, d).wait_recv()
            acc = acc + yrecv[h, d].astype(F32)
        ride, body = regate(acc, part_rows)
        acc = jnp.where(body, acc, ride).astype(BF)
        rsend[h * blocks:(h + 1) * blocks] = dot(place, acc).astype(BF).reshape(blocks, 16, LANE)

        def rzstart(j, carry):
            target = h * blocks + j

            @pl.when(target != z)
            def _():
                rzcopy(lax.rem(target + NZ - z, NZ)).start()

            return carry

        lax.fori_loop(0, blocks, rzstart, 0)
    rrecv[z] = rsend[z]

    def rzwait(d, carry):
        rzcopy(d).wait_recv()
        return carry

    lax.fori_loop(1, NZ, rzwait, 0)
    out = jnp.zeros((TOK, LANE), F32)
    gout = [jnp.zeros((TOK, 1), F32) for _ in range(4)]
    for e in range(NZ // 2):
        hits = [chosen[k] == e for k in range(4)]
        w = jnp.zeros((TOK, 1), F32)
        for k in range(4):
            w = w + jnp.where(hits[k], weight[k], 0.0)
        v = rrecv[2 * e].astype(F32) + rrecv[2 * e + 1].astype(F32)
        v = v[0:TOK]
        out = out + w * v
        gate = v[:, FEAT:FEAT + 1] + v[:, FEAT + 1:FEAT + 2]
        gout = [gout[k] + jnp.where(hits[k], gate, 0.0) for k in range(4)]
    tg_out[...] = out[:, 0:FEAT].astype(BF)
    for k in range(4):
        gg_out[k:k + 1, :] = jnp.sum(jnp.where(small, gout[k], 0.0), axis=0, keepdims=True)

    def zdone(d, carry):
        zcopy(d).wait_send()
        rzcopy(d).wait_send()
        return carry

    lax.fori_loop(1, NZ, zdone, 0)
    wsend.wait_send()
    for cp in (psend, tswap, gswap):
        cp.wait_send()
    for d in range(1, NX):
        xcopy(d).wait_send()
    for h in (0, 1):
        for way in (0, 1):
            s1copy(h, way).wait_send()
            s2copy(h, way).wait_send()
        for d in range(1, NY):
            rycopy(h, d).wait_send()
    for s in range(4):
        for i in range(NX):
            for way in (0, 1):
                ycopy(i, s, way).wait_send()


def body(tokens, out_grad, expert_ids, gate_probs, w_gate, w_up, w_down):
    vmem = pl.BlockSpec(memory_space=pltpu.VMEM)
    hbm = pl.BlockSpec(memory_space=pltpu.HBM)
    dma = pltpu.SemaphoreType.DMA
    token_grad, gate_grad = pl.pallas_call(
        kernel,
        out_shape=(
            jax.ShapeDtypeStruct((TOK, FEAT), BF),
            jax.ShapeDtypeStruct((4, TOK), F32),
        ),
        in_specs=[hbm] * 7,
        out_specs=(vmem, vmem),
        scratch_shapes=[
            pltpu.VMEM((2, TOK, FEAT), BF),
            pltpu.VMEM((4, TOK), jnp.int32),
            pltpu.VMEM((4, TOK), F32),
            pltpu.VMEM((3, HID, SLICES * 2 * FEAT), BF),
            pltpu.VMEM((2, 3, HPAD, SLICES * LANE), BF),
            pltpu.VMEM((3, 2, HPAD, SLICES * LANE), BF),
            pltpu.VMEM((32, LANE), BF),
            pltpu.VMEM((NZ, 32, LANE), BF),
            pltpu.VMEM((SLICES, LANE, COLS), BF),
            pltpu.VMEM((3, 2, HPAD, 256), F32),
            pltpu.VMEM((3, HPAD, 256), F32),
            pltpu.VMEM((2, 2, HPAD, 256), BF),
            pltpu.VMEM((8, 256), F32),
            pltpu.VMEM((8, 256), F32),
            pltpu.VMEM((2, 2, ROWS // 4, WIDE), BF),
            pltpu.VMEM((2, 2, ROWS // 4, WIDE), BF),
            pltpu.VMEM((2, 2, ROWS // 2, WIDE), BF),
            pltpu.VMEM((2, 2, ROWS // 2, WIDE), BF),
            pltpu.VMEM((2, NY, ROWS // 2, LANE), BF),
            pltpu.VMEM((2, NY, ROWS // 2, LANE), BF),
            pltpu.VMEM((NZ, 16, LANE), BF),
            pltpu.VMEM((NZ, 16, LANE), BF),
            dma((4,)),
            dma((3,)),
            dma((1,)),
            dma((2,)),
            dma((6,)),
            dma((NZ,)), dma((NZ,)),
            dma((NX,)), dma((NX,)),
            dma((2, NX, 4)), dma((2, NX, 4)),
            dma((2, 2)), dma((2, 2)),
            dma((2, 2)), dma((2, 2)),
            dma((2, NY)), dma((2, NY)),
            dma((NZ,)), dma((NZ,)),
        ],
        compiler_params=pltpu.CompilerParams(
            collective_id=0, has_side_effects=True, vmem_limit_bytes=63 * 2**20
        ),
    )(tokens, out_grad, expert_ids.T, gate_probs.T, w_gate, w_up, w_down)
    return token_grad, gate_grad.T


def solution(mesh):
    in_specs = (
        P("expert", "tensor"),
        P("expert", "tensor"),
        P("expert", None),
        P("expert", None),
        P("expert", "tensor", None),
        P("expert", "tensor", None),
        P("expert", "tensor", None),
    )
    out_specs = (P("expert", "tensor"), P("expert", None))
    return jax.shard_map(body, mesh=mesh, in_specs=in_specs, out_specs=out_specs, check_vma=False)
```

```python
import jax
import jax.numpy as jnp
from jax import lax
from jax.experimental import pallas as pl
from jax.experimental.pallas import tpu as pltpu
from jax.sharding import PartitionSpec as P

MESH = pl.DeviceIdType.MESH
BF = jnp.bfloat16
F32 = jnp.float32
NZ, NY, NX = 16, 8, 4
SLICES = NY * NX
HID = 84
HPAD = 96
FEAT = 96
LANE = 128
TOK = 12
ROWS = NZ * TOK
WIDE = NX * LANE


def iota(shape, dim):
    return lax.broadcasted_iota(jnp.int32, shape, dim)


def dot(a, b, ca=1, cb=0):
    return lax.dot_general(a, b, (((ca,), (cb,)), ((), ())), preferred_element_type=F32)


def kernel(
    tok, grad, ids_in, probs_in, wg, wu, wd,
    tg_out, gg_out,
    tin, ids, probs, wraw, wr, wall, zsend, zbuf, xnear, xrest, part, part2, gcat, tmine, tother,
    bwd, xs1, xr1, xs2, xr2, ysend, yrecv, rsend, rrecv,
    tsem, wsem, lsem, ssem, csem,
    zss, zrs, yss, yrs, x1s, x1r, x2s, x2r, s1s, s1r, s2s, s2r, rys, ryr, rzs, rzr,
):
    z = lax.axis_index("expert")
    t = lax.axis_index("tensor")
    y = t // 8
    x = lax.rem(t // 2, 4)
    c = lax.rem(t, 2)
    other = 1 - c

    def dev(zz, yy, xx, cc):
        return (zz, (yy * NX + xx) * 2 + cc)

    def zdev(d):
        return dev(lax.rem(z + d, NZ), y, x, c)

    def ydev(d):
        return dev(z, lax.rem(y + d, NY), x, c)

    def xdev(d):
        return dev(z, y, lax.rem(x + d, NX), c)

    sibling = dev(z, y, x, other)

    def remote(src, dst, ss, rs, target):
        return pltpu.make_async_remote_copy(
            src_ref=src, dst_ref=dst, send_sem=ss, recv_sem=rs, device_id=target, device_id_type=MESH
        )

    bar = pltpu.get_barrier_semaphore()

    def greet_z(d, carry):
        pl.semaphore_signal(bar, inc=1, device_id=zdev(d), device_id_type=MESH)
        return carry

    def greet_y(d, carry):
        pl.semaphore_signal(bar, inc=1, device_id=ydev(d), device_id_type=MESH)
        return carry

    def greet_x(d, carry):
        pl.semaphore_signal(bar, inc=1, device_id=xdev(d), device_id_type=MESH)
        return carry

    lax.fori_loop(1, NZ, greet_z, 0)
    lax.fori_loop(1, NY, greet_y, 0)
    lax.fori_loop(1, NX, greet_x, 0)
    pl.semaphore_signal(bar, inc=1, device_id=sibling, device_id_type=MESH)

    heads = [pltpu.make_async_copy(src, tin.at[i], tsem.at[i]) for i, src in enumerate((tok, grad))]
    heads.append(pltpu.make_async_copy(ids_in, ids, tsem.at[2]))
    heads.append(pltpu.make_async_copy(probs_in, probs, tsem.at[3]))
    for cp in heads:
        cp.start()
    loads = [
        pltpu.make_async_copy(src.at[0], wraw.at[i], wsem.at[i]) for i, src in enumerate((wg, wu, wd))
    ]
    for cp in loads:
        cp.start()

    zsend[...] = jnp.zeros_like(zsend)
    for cp in heads:
        cp.wait()
    zsend[0:TOK, 0:FEAT] = tin[0]
    zsend[16:16 + TOK, 0:FEAT] = tin[1]
    zbuf[0] = zsend[...]

    pl.semaphore_wait(bar, (NZ - 1) + (NY - 1) + (NX - 1) + 1)

    def place_of(d):
        return 2 * d - 1 if 0 < d < 8 else (2 * (NZ - d) if d > 8 else (15 if d else 0))

    z_order = (1, 15, 2, 14, 3, 13, 4, 12, 5, 11, 6, 10, 7, 9, 8)

    def zcopy(d):
        return remote(zsend, zbuf.at[place_of(NZ - d)], zss.at[d], zrs.at[d], zdev(d))

    for d in z_order:
        zcopy(d).start()

    xnear[:, FEAT:LANE, :] = jnp.zeros((SLICES, LANE - FEAT, LANE), BF)
    xrest[:, FEAT:LANE, :] = jnp.zeros((SLICES, LANE - FEAT, 2 * LANE), BF)
    wr[:, :, 80:HPAD, :] = jnp.zeros((2, 3, HPAD - 80, SLICES * LANE), BF)
    row = iota((4 * FEAT, 4 * LANE), 0)
    q = (
        (row >= FEAT).astype(jnp.int32)
        + (row >= 2 * FEAT).astype(jnp.int32)
        + (row >= 3 * FEAT).astype(jnp.int32)
    )
    spread = jnp.where(iota((4 * FEAT, 4 * LANE), 1) == row + q * (LANE - FEAT), 1.0, 0.0).astype(BF)
    for cp in loads:
        cp.wait()

    def relay(g, carry):
        yy = g // 2
        xx = 2 * lax.rem(g, 2)
        for i in range(3):
            wide = dot(
                wraw[i, :, pl.ds(pl.multiple_of(g * (4 * FEAT), LANE), 4 * FEAT)], spread
            ).astype(BF)
            for j in range(4):
                at = pl.multiple_of((yy * NX + xx + j // 2) * LANE, LANE)
                wr[j % 2, i, 0:HID, pl.ds(at, LANE)] = wide[:, j * LANE:(j + 1) * LANE]
        return carry

    lax.fori_loop(0, 16, relay, 0)
    wsend = remote(wr.at[other], wall.at[:, c], ssem.at[0], ssem.at[1], sibling)
    wsend.start()
    wown = pltpu.make_async_copy(wr.at[c], wall.at[:, c], lsem.at[0])
    wown.start()

    small = iota((TOK, TOK), 0) == iota((TOK, TOK), 1)

    def upright(ref, k, zero):
        return jnp.sum(jnp.where(small, ref[k:k + 1, :], zero), axis=1, keepdims=True)

    chosen = [upright(ids, k, 0) for k in range(4)]
    weight = [upright(probs, k, 0.0) for k in range(4)]

    slot = y * NX + x
    bufs = (xnear, xrest)
    counts = (64, ROWS - 64)
    spans = ((0, 6), (5, NZ))

    def turn(g):
        first, end = spans[g]
        shape = ((end - first) * 32, 2 * counts[g])
        r = iota(shape, 0)
        p = ((r >> 5) + first) * TOK + (r & 15) - 64 * g
        col = ((r >> 4) & 1) * counts[g] + p
        fit = (p >= 0) & (p < counts[g]) & ((r & 15) < TOK) & (iota(shape, 1) == col)
        rows = zbuf[first:end].reshape(shape[0], LANE)
        mine = dot(rows, jnp.where(fit, 1.0, 0.0).astype(BF), 0, 0).astype(BF)
        bufs[g][slot, 0:FEAT, :] = mine[0:FEAT, :]

    half = FEAT // 2
    nextx = (xdev(1), xdev(NX - 1))
    near_first = (1, 7, 2, 6, 3, 5, 4)
    blocks_in = (0,) + near_first

    def ycopy(g, d):
        ref = bufs[g].at[slot, pl.ds(0, FEAT)]
        return remote(ref, ref, yss.at[g, d], yrs.at[g, d], ydev(d))

    def x1copy(g, d, way):
        ref = bufs[g].at[lax.rem(y + NY - d, NY) * NX + x, pl.ds(0, FEAT)]
        return remote(ref, ref, x1s.at[g, d, way], x1r.at[g, d, way], nextx[way])

    def x2copy(g, d, way):
        xx = lax.rem(x + (NX - 1 if way == 0 else 1), NX)
        ref = bufs[g].at[lax.rem(y + NY - d, NY) * NX + xx, pl.ds(way * half, half)]
        return remote(ref, ref, x2s.at[g, d, way], x2r.at[g, d, way], nextx[way])

    def launch(g):
        turn(g)
        for way in (0, 1):
            x1copy(g, 0, way).start()
        for d in near_first:
            ycopy(g, d).start()

    def across(g, ds):
        for d in ds:
            ycopy(g, d).wait_recv()
            for way in (0, 1):
                x1copy(g, d, way).start()

    def onward(g):
        for d in blocks_in:
            for way in (0, 1):
                x1copy(g, d, way).wait_recv()
                x2copy(g, d, way).start()

    early = (15, 1, 14, 2, 13)
    for d in early:
        zcopy(d).wait_recv()
    launch(0)
    across(0, near_first[:4])
    for d in z_order:
        if d not in early:
            zcopy(d).wait_recv()
    launch(1)
    across(0, near_first[4:])
    onward(0)
    across(1, near_first)
    onward(1)

    def forward(d, cores):
        yy = lax.rem(y + NY - d, NY)
        lanes = pl.ds(pl.multiple_of(yy * WIDE, LANE), WIDE)
        near = xnear[pl.ds(yy * NX, NX)].reshape(WIDE, LANE)
        rest = xrest[pl.ds(yy * NX, NX)].reshape(WIDE, 2 * LANE)
        toks = jnp.concatenate([near, rest[:, 0:LANE]], axis=1)
        grads = jnp.concatenate([near, rest[:, LANE:2 * LANE]], axis=1)
        for cc in cores:
            pair = wall[0:2, cc, :, lanes].reshape(2 * HPAD, WIDE)
            pair = dot(pair, toks).reshape(2, HPAD, 256)
            down = dot(wall[2, cc, :, lanes], grads)
            if d == 0:
                part[0:2, cc] = pair
                part[2, cc] = down
            else:
                part[0:2, cc] += pair
                part[2, cc] += down

    wown.wait()
    wsend.wait_recv()
    for d in blocks_in:
        for g in (0, 1):
            for way in (0, 1):
                x2copy(g, d, way).wait_recv()
        if d != 4:
            forward(d, (0, 1))
    forward(4, (other,))
    psend = remote(part.at[:, other], part2, csem.at[0], csem.at[1], sibling)
    psend.start()
    forward(4, (c,))
    psend.wait_recv()

    def tokens_of(v):
        return jnp.concatenate([v[:, 0:64], v[:, LANE:2 * LANE]], axis=1)

    pre_gate = tokens_of(part[0, c] + part2[0])
    pre_up = tokens_of(part[1, c] + part2[1])
    back = (part[2, c] + part2[2])[:, 64:64 + ROWS]
    sig = jax.nn.sigmoid(pre_gate)
    act = pre_gate * sig
    slope = sig * (1.0 + pre_gate * (1.0 - sig))
    hidden = (act * pre_up).astype(BF).astype(F32)
    terms = jnp.sum(hidden * back, axis=0, keepdims=True)
    tmine[:, 0:ROWS] = jnp.broadcast_to(terms, (8, ROWS))
    gcat[0, c, :, 0:ROWS] = (back * pre_up * slope).astype(BF)
    gcat[1, c, :, 0:ROWS] = (back * act).astype(BF)
    tswap = remote(tmine, tother, csem.at[2], csem.at[3], sibling)
    tswap.start()
    gswap = remote(gcat.at[:, c], gcat.at[:, c], csem.at[4], csem.at[5], sibling)
    gswap.start()

    def gate_lanes(column, rows):
        hi = column.astype(BF).astype(F32)
        lane = iota((rows, LANE), 1)
        return jnp.where(lane == FEAT, hi, jnp.where(lane == FEAT + 1, column - hi, 0.0))

    def regate(v, rows):
        lane = iota((rows, LANE), 1)
        gate = jnp.sum(
            jnp.where((lane == FEAT) | (lane == FEAT + 1), v, 0.0), axis=1, keepdims=True
        )
        return gate_lanes(gate, rows), lane < FEAT

    def sealed(v, rows):
        ride, body = regate(v, rows)
        return jnp.where(body, v, ride).astype(BF)

    eye = iota((ROWS, ROWS), 0) == iota((ROWS, ROWS), 1)
    tswap.wait_recv()
    terms = terms + tother[0:1, 0:ROWS]
    column = jnp.sum(jnp.where(eye, terms, 0.0), axis=1, keepdims=True)
    ride = jnp.concatenate([gate_lanes(column, ROWS)] * NX, axis=1)
    gswap.wait_recv()
    gt = gcat[...].reshape(4 * HPAD, 256)[:, 0:ROWS]

    far_first = (4, 3, 5, 2, 6, 1, 7, 0)
    part_rows = ROWS // 2

    def s1copy(d, way):
        return remote(xs1.at[d, way], xr1.at[d, way], s1s.at[d, way], s1r.at[d, way], nextx[way])

    def s2copy(d, way):
        return remote(xs2.at[d, way], xr2.at[d, way], s2s.at[d, way], s2r.at[d, way], nextx[way])

    def xlanes(k):
        return pl.ds(pl.multiple_of(lax.rem(x + k, NX) * LANE, LANE), LANE)

    for d in far_first:
        lanes = pl.ds(pl.multiple_of(lax.rem(y + d, NY) * WIDE, LANE), WIDE)
        bwd[d] = dot(gt, wall[0:2, :, :, lanes].reshape(4 * HPAD, WIDE), 0, 0) + ride
        for way in (0, 1):
            rows = pl.ds(way * part_rows, part_rows)
            xs1[d, way] = bwd[d, rows, xlanes(2)].astype(BF)
            s1copy(d, way).start()
    for d in far_first:
        for way in (0, 1):
            near = xlanes(1 if way == 0 else NX - 1)
            rest = pl.ds((1 - way) * part_rows, part_rows)
            xs2[d, way, rest, :] = bwd[d, rest, near].astype(BF)
            rows = pl.ds(way * part_rows, part_rows)
            s1copy(d, way).wait_recv()
            mine = bwd[d, rows, near] + xr1[d, way].astype(F32)
            xs2[d, way, rows, :] = sealed(mine, part_rows)
            s2copy(d, way).start()

    def rycopy(d):
        return remote(ysend.at[d], yrecv.at[d], rys.at[d], ryr.at[d], ydev(d))

    for d in far_first:
        v = bwd[d, :, xlanes(0)]
        for way in (0, 1):
            s2copy(d, way).wait_recv()
            v = v + xr2[d, way].astype(F32)
        if d:
            ysend[d] = sealed(v, ROWS)
            rycopy(d).start()
        else:
            acc = v

    for d in far_first[:NY - 1]:
        rycopy(d).wait_recv()
        acc = acc + yrecv[d].astype(F32)
    r = iota((NZ * 16, ROWS), 0)
    place = (iota((NZ * 16, ROWS), 1) == (r >> 4) * TOK + (r & 15)) & ((r & 15) < TOK)
    place = jnp.where(place, 1.0, 0.0).astype(BF)
    rsend[...] = dot(place, sealed(acc, ROWS)).astype(BF).reshape(NZ, 16, LANE)
    rrecv[z] = rsend[0]

    def rzcopy(d):
        return remote(rsend.at[place_of(d)], rrecv.at[z], rzs.at[d], rzr.at[d], zdev(d))

    for d in z_order[::-1]:
        rzcopy(d).start()

    for d in z_order:
        rzcopy(d).wait_recv()
    out = jnp.zeros((TOK, LANE), F32)
    gout = [jnp.zeros((TOK, 1), F32) for _ in range(4)]
    for e in range(NZ // 2):
        hits = [chosen[k] == e for k in range(4)]
        w = jnp.zeros((TOK, 1), F32)
        for k in range(4):
            w = w + jnp.where(hits[k], weight[k], 0.0)
        v = rrecv[2 * e].astype(F32) + rrecv[2 * e + 1].astype(F32)
        v = v[0:TOK]
        out = out + w * v
        gate = v[:, FEAT:FEAT + 1] + v[:, FEAT + 1:FEAT + 2]
        gout = [gout[k] + jnp.where(hits[k], gate, 0.0) for k in range(4)]
    tg_out[...] = out[:, 0:FEAT].astype(BF)
    for k in range(4):
        gg_out[k:k + 1, :] = jnp.sum(jnp.where(small, gout[k], 0.0), axis=0, keepdims=True)

    for d in z_order:
        zcopy(d).wait_send()
        rzcopy(d).wait_send()
    wsend.wait_send()
    for cp in (psend, tswap, gswap):
        cp.wait_send()
    for d in range(NY):
        if d:
            rycopy(d).wait_send()
            for g in (0, 1):
                ycopy(g, d).wait_send()
        for way in (0, 1):
            for g in (0, 1):
                x1copy(g, d, way).wait_send()
                x2copy(g, d, way).wait_send()
            s1copy(d, way).wait_send()
            s2copy(d, way).wait_send()


def body(tokens, out_grad, expert_ids, gate_probs, w_gate, w_up, w_down):
    vmem = pl.BlockSpec(memory_space=pltpu.VMEM)
    hbm = pl.BlockSpec(memory_space=pltpu.HBM)
    dma = pltpu.SemaphoreType.DMA
    token_grad, gate_grad = pl.pallas_call(
        kernel,
        out_shape=(
            jax.ShapeDtypeStruct((TOK, FEAT), BF),
            jax.ShapeDtypeStruct((4, TOK), F32),
        ),
        in_specs=[hbm] * 7,
        out_specs=(vmem, vmem),
        scratch_shapes=[
            pltpu.VMEM((2, TOK, FEAT), BF),
            pltpu.VMEM((4, TOK), jnp.int32),
            pltpu.VMEM((4, TOK), F32),
            pltpu.VMEM((3, HID, SLICES * 2 * FEAT), BF),
            pltpu.VMEM((2, 3, HPAD, SLICES * LANE), BF),
            pltpu.VMEM((3, 2, HPAD, SLICES * LANE), BF),
            pltpu.VMEM((32, LANE), BF),
            pltpu.VMEM((NZ, 32, LANE), BF),
            pltpu.VMEM((SLICES, LANE, LANE), BF),
            pltpu.VMEM((SLICES, LANE, 2 * LANE), BF),
            pltpu.VMEM((3, 2, HPAD, 256), F32),
            pltpu.VMEM((3, HPAD, 256), F32),
            pltpu.VMEM((2, 2, HPAD, 256), BF),
            pltpu.VMEM((8, 256), F32),
            pltpu.VMEM((8, 256), F32),
            pltpu.VMEM((NY, ROWS, WIDE), F32),
            pltpu.VMEM((NY, 2, ROWS // 2, LANE), BF),
            pltpu.VMEM((NY, 2, ROWS // 2, LANE), BF),
            pltpu.VMEM((NY, 2, ROWS, LANE), BF),
            pltpu.VMEM((NY, 2, ROWS, LANE), BF),
            pltpu.VMEM((NY, ROWS, LANE), BF),
            pltpu.VMEM((NY, ROWS, LANE), BF),
            pltpu.VMEM((NZ, 16, LANE), BF),
            pltpu.VMEM((NZ, 16, LANE), BF),
            dma((4,)),
            dma((3,)),
            dma((1,)),
            dma((2,)),
            dma((6,)),
            dma((NZ,)), dma((NZ,)),
            dma((2, NY)), dma((2, NY)),
            dma((2, NY, 2)), dma((2, NY, 2)),
            dma((2, NY, 2)), dma((2, NY, 2)),
            dma((NY, 2)), dma((NY, 2)),
            dma((NY, 2)), dma((NY, 2)),
            dma((NY,)), dma((NY,)),
            dma((NZ,)), dma((NZ,)),
        ],
        compiler_params=pltpu.CompilerParams(
            collective_id=0, has_side_effects=True, vmem_limit_bytes=63 * 2**20
        ),
    )(tokens, out_grad, expert_ids.T, gate_probs.T, w_gate, w_up, w_down)
    return token_grad, gate_grad.T


def solution(mesh):
    in_specs = (
        P("expert", "tensor"),
        P("expert", "tensor"),
        P("expert", None),
        P("expert", None),
        P("expert", "tensor", None),
        P("expert", "tensor", None),
        P("expert", "tensor", None),
    )
    out_specs = (P("expert", "tensor"), P("expert", None))
    return jax.shard_map(body, mesh=mesh, in_specs=in_specs, out_specs=out_specs, check_vma=False)
```

```python
import jax
import jax.numpy as jnp
from jax import lax
from jax.experimental import pallas as pl
from jax.experimental.pallas import tpu as pltpu
from jax.sharding import PartitionSpec as P

MESH = pl.DeviceIdType.MESH
BF = jnp.bfloat16
F32 = jnp.float32
NZ, NY, NX = 16, 8, 4
SLICES = NY * NX
HID = 84
HPAD = 96
FEAT = 96
LANE = 128
TOK = 12
ROWS = NZ * TOK
WIDE = NX * LANE


def iota(shape, dim):
    return lax.broadcasted_iota(jnp.int32, shape, dim)


def dot(a, b, ca=1, cb=0):
    return lax.dot_general(a, b, (((ca,), (cb,)), ((), ())), preferred_element_type=F32)


def kernel(
    tok, grad, ids_in, probs_in, wg, wu, wd,
    tg_out, gg_out,
    tin, ids, probs, wraw, wr, wall, zsend, zbuf, xnear, xrest, part, part2, gcat, tmine, tother,
    bwd, xs1, xr1, xs2, xr2, ysend, yrecv, rsend, rrecv,
    tsem, wsem, lsem, ssem, csem,
    zss, zrs, yss, yrs, x1s, x1r, x2s, x2r, s1s, s1r, s2s, s2r, rys, ryr, rzs, rzr,
):
    z = lax.axis_index("expert")
    t = lax.axis_index("tensor")
    y = t // 8
    x = lax.rem(t // 2, 4)
    c = lax.rem(t, 2)
    other = 1 - c

    def dev(zz, yy, xx, cc):
        return (zz, (yy * NX + xx) * 2 + cc)

    def zdev(d):
        return dev(lax.rem(z + d, NZ), y, x, c)

    def ydev(d):
        return dev(z, lax.rem(y + d, NY), x, c)

    def xdev(d):
        return dev(z, y, lax.rem(x + d, NX), c)

    sibling = dev(z, y, x, other)

    def remote(src, dst, ss, rs, target):
        return pltpu.make_async_remote_copy(
            src_ref=src, dst_ref=dst, send_sem=ss, recv_sem=rs, device_id=target, device_id_type=MESH
        )

    bar = pltpu.get_barrier_semaphore()

    def greet_z(d, carry):
        pl.semaphore_signal(bar, inc=1, device_id=zdev(d), device_id_type=MESH)
        return carry

    def greet_y(d, carry):
        pl.semaphore_signal(bar, inc=1, device_id=ydev(d), device_id_type=MESH)
        return carry

    def greet_x(d, carry):
        pl.semaphore_signal(bar, inc=1, device_id=xdev(d), device_id_type=MESH)
        return carry

    lax.fori_loop(1, NZ, greet_z, 0)
    lax.fori_loop(1, NY, greet_y, 0)
    lax.fori_loop(1, NX, greet_x, 0)
    pl.semaphore_signal(bar, inc=1, device_id=sibling, device_id_type=MESH)

    heads = [pltpu.make_async_copy(src, tin.at[i], tsem.at[i]) for i, src in enumerate((tok, grad))]
    heads.append(pltpu.make_async_copy(ids_in, ids, tsem.at[2]))
    heads.append(pltpu.make_async_copy(probs_in, probs, tsem.at[3]))
    for cp in heads:
        cp.start()
    loads = [
        pltpu.make_async_copy(src.at[0], wraw.at[i], wsem.at[i]) for i, src in enumerate((wg, wu, wd))
    ]
    for cp in loads:
        cp.start()

    zsend[...] = jnp.zeros_like(zsend)
    for cp in heads:
        cp.wait()
    zsend[0:TOK, 0:FEAT] = tin[0]
    zsend[16:16 + TOK, 0:FEAT] = tin[1]
    zbuf[0] = zsend[...]

    pl.semaphore_wait(bar, (NZ - 1) + (NY - 1) + (NX - 1) + 1)

    def place_of(d):
        return 2 * d - 1 if 0 < d < 8 else (2 * (NZ - d) if d > 8 else (15 if d else 0))

    z_order = (1, 15, 2, 14, 3, 13, 4, 12, 5, 11, 6, 10, 7, 9, 8)

    def zcopy(d):
        return remote(zsend, zbuf.at[place_of(NZ - d)], zss.at[d], zrs.at[d], zdev(d))

    for d in z_order:
        zcopy(d).start()

    xnear[:, FEAT:LANE, :] = jnp.zeros((SLICES, LANE - FEAT, LANE), BF)
    xrest[:, FEAT:LANE, :] = jnp.zeros((SLICES, LANE - FEAT, 2 * LANE), BF)
    wr[:, :, 80:HPAD, :] = jnp.zeros((2, 3, HPAD - 80, SLICES * LANE), BF)
    row = iota((4 * FEAT, 4 * LANE), 0)
    q = (
        (row >= FEAT).astype(jnp.int32)
        + (row >= 2 * FEAT).astype(jnp.int32)
        + (row >= 3 * FEAT).astype(jnp.int32)
    )
    spread = jnp.where(iota((4 * FEAT, 4 * LANE), 1) == row + q * (LANE - FEAT), 1.0, 0.0).astype(BF)
    for cp in loads:
        cp.wait()

    def relay(g, carry):
        yy = g // 2
        xx = 2 * lax.rem(g, 2)
        for i in range(3):
            wide = dot(
                wraw[i, :, pl.ds(pl.multiple_of(g * (4 * FEAT), LANE), 4 * FEAT)], spread
            ).astype(BF)
            for j in range(4):
                at = pl.multiple_of((yy * NX + xx + j // 2) * LANE, LANE)
                wr[j % 2, i, 0:HID, pl.ds(at, LANE)] = wide[:, j * LANE:(j + 1) * LANE]
        return carry

    lax.fori_loop(0, 16, relay, 0)
    wsend = remote(wr.at[other], wall.at[:, c], ssem.at[0], ssem.at[1], sibling)
    wsend.start()
    wown = pltpu.make_async_copy(wr.at[c], wall.at[:, c], lsem.at[0])
    wown.start()

    small = iota((TOK, TOK), 0) == iota((TOK, TOK), 1)

    def upright(ref, k, zero):
        return jnp.sum(jnp.where(small, ref[k:k + 1, :], zero), axis=1, keepdims=True)

    chosen = [upright(ids, k, 0) for k in range(4)]
    weight = [upright(probs, k, 0.0) for k in range(4)]

    slot = y * NX + x
    bufs = (xnear, xrest)
    counts = (64, ROWS - 64)
    spans = ((0, 6), (5, NZ))

    def turn(g):
        first, end = spans[g]
        shape = ((end - first) * 32, 2 * counts[g])
        r = iota(shape, 0)
        p = ((r >> 5) + first) * TOK + (r & 15) - 64 * g
        col = ((r >> 4) & 1) * counts[g] + p
        fit = (p >= 0) & (p < counts[g]) & ((r & 15) < TOK) & (iota(shape, 1) == col)
        rows = zbuf[first:end].reshape(shape[0], LANE)
        mine = dot(rows, jnp.where(fit, 1.0, 0.0).astype(BF), 0, 0).astype(BF)
        bufs[g][slot, 0:FEAT, :] = mine[0:FEAT, :]

    half = FEAT // 2
    nextx = (xdev(1), xdev(NX - 1))
    near_first = (1, 7, 2, 6, 3, 5, 4)
    blocks_in = (0,) + near_first

    def ycopy(g, d):
        ref = bufs[g].at[slot, pl.ds(0, FEAT)]
        return remote(ref, ref, yss.at[g, d], yrs.at[g, d], ydev(d))

    def x1copy(g, d, way):
        ref = bufs[g].at[lax.rem(y + NY - d, NY) * NX + x, pl.ds(0, FEAT)]
        return remote(ref, ref, x1s.at[g, d, way], x1r.at[g, d, way], nextx[way])

    def x2copy(g, d, way):
        xx = lax.rem(x + (NX - 1 if way == 0 else 1), NX)
        ref = bufs[g].at[lax.rem(y + NY - d, NY) * NX + xx, pl.ds(way * half, half)]
        return remote(ref, ref, x2s.at[g, d, way], x2r.at[g, d, way], nextx[way])

    def launch(g):
        turn(g)
        for way in (0, 1):
            x1copy(g, 0, way).start()
        for d in near_first:
            ycopy(g, d).start()

    def across(g, ds):
        for d in ds:
            ycopy(g, d).wait_recv()
            for way in (0, 1):
                x1copy(g, d, way).start()

    def onward(g):
        for d in blocks_in:
            for way in (0, 1):
                x1copy(g, d, way).wait_recv()
                x2copy(g, d, way).start()

    early = (15, 1, 14, 2, 13)
    for d in early:
        zcopy(d).wait_recv()
    launch(0)
    across(0, near_first[:4])
    for d in z_order:
        if d not in early:
            zcopy(d).wait_recv()
    launch(1)
    across(0, near_first[4:])
    onward(0)
    across(1, near_first)
    onward(1)

    def forward(d, cores):
        yy = lax.rem(y + NY - d, NY)
        lanes = pl.ds(pl.multiple_of(yy * WIDE, LANE), WIDE)
        near = xnear[pl.ds(yy * NX, NX)].reshape(WIDE, LANE)
        rest = xrest[pl.ds(yy * NX, NX)].reshape(WIDE, 2 * LANE)
        toks = jnp.concatenate([near, rest[:, 0:LANE]], axis=1)
        grads = jnp.concatenate([near, rest[:, LANE:2 * LANE]], axis=1)
        for cc in cores:
            pair = wall[0:2, cc, :, lanes].reshape(2 * HPAD, WIDE)
            pair = dot(pair, toks).reshape(2, HPAD, 256)
            down = dot(wall[2, cc, :, lanes], grads)
            if d == 0:
                part[0:2, cc] = pair
                part[2, cc] = down
            else:
                part[0:2, cc] += pair
                part[2, cc] += down

    wown.wait()
    wsend.wait_recv()
    for d in blocks_in:
        for g in (0, 1):
            for way in (0, 1):
                x2copy(g, d, way).wait_recv()
        if d != 4:
            forward(d, (0, 1))
    forward(4, (other,))
    psend = remote(part.at[:, other], part2, csem.at[0], csem.at[1], sibling)
    psend.start()
    forward(4, (c,))
    psend.wait_recv()

    def tokens_of(v):
        return jnp.concatenate([v[:, 0:64], v[:, LANE:2 * LANE]], axis=1)

    pre_gate = tokens_of(part[0, c] + part2[0])
    pre_up = tokens_of(part[1, c] + part2[1])
    back = (part[2, c] + part2[2])[:, 64:64 + ROWS]
    sig = jax.nn.sigmoid(pre_gate)
    act = pre_gate * sig
    slope = sig * (1.0 + pre_gate * (1.0 - sig))
    hidden = (act * pre_up).astype(BF).astype(F32)
    terms = jnp.sum(hidden * back, axis=0, keepdims=True)
    tmine[:, 0:ROWS] = jnp.broadcast_to(terms, (8, ROWS))
    gcat[0, c, :, 0:ROWS] = (back * pre_up * slope).astype(BF)
    gcat[1, c, :, 0:ROWS] = (back * act).astype(BF)
    tswap = remote(tmine, tother, csem.at[2], csem.at[3], sibling)
    tswap.start()
    gswap = remote(gcat.at[:, c], gcat.at[:, c], csem.at[4], csem.at[5], sibling)
    gswap.start()

    def gate_lanes(column, rows):
        hi = column.astype(BF).astype(F32)
        lane = iota((rows, LANE), 1)
        return jnp.where(lane == FEAT, hi, jnp.where(lane == FEAT + 1, column - hi, 0.0))

    def regate(v, rows):
        lane = iota((rows, LANE), 1)
        gate = jnp.sum(
            jnp.where((lane == FEAT) | (lane == FEAT + 1), v, 0.0), axis=1, keepdims=True
        )
        return gate_lanes(gate, rows), lane < FEAT

    def sealed(v, rows):
        ride, body = regate(v, rows)
        return jnp.where(body, v, ride).astype(BF)

    eye = iota((ROWS, ROWS), 0) == iota((ROWS, ROWS), 1)
    tswap.wait_recv()
    terms = terms + tother[0:1, 0:ROWS]
    column = jnp.sum(jnp.where(eye, terms, 0.0), axis=1, keepdims=True)
    ride = jnp.concatenate([gate_lanes(column, ROWS)] * NX, axis=1)
    gswap.wait_recv()
    gt = gcat[...].reshape(4 * HPAD, 256)[:, 0:ROWS]

    far_first = (4, 3, 5, 2, 6, 1, 7, 0)
    bases = (0, 64)

    def s1copy(g, d, way):
        at = pl.ds(bases[g] // 2, counts[g] // 2)
        return remote(
            xs1.at[d, way, at], xr1.at[d, way, at], s1s.at[g, d, way], s1r.at[g, d, way], nextx[way]
        )

    def s2copy(g, d, way):
        at = pl.ds(bases[g], counts[g])
        return remote(
            xs2.at[d, way, at], xr2.at[d, way, at], s2s.at[g, d, way], s2r.at[g, d, way], nextx[way]
        )

    def xlanes(k):
        return pl.ds(pl.multiple_of(lax.rem(x + k, NX) * LANE, LANE), LANE)

    def first_step(g, d):
        n = counts[g] // 2
        for way in (0, 1):
            rows = pl.ds(bases[g] + way * n, n)
            xs1[d, way, pl.ds(bases[g] // 2, n), :] = bwd[d, rows, xlanes(2)].astype(BF)
            s1copy(g, d, way).start()

    for d in far_first:
        lanes = pl.ds(pl.multiple_of(lax.rem(y + d, NY) * WIDE, LANE), WIDE)
        bwd[d] = dot(gt, wall[0:2, :, :, lanes].reshape(4 * HPAD, WIDE), 0, 0) + ride
        first_step(1, d)
    for d in far_first:
        first_step(0, d)
    for g in (1, 0):
        n = counts[g] // 2
        for d in far_first:
            for way in (0, 1):
                near = xlanes(1 if way == 0 else NX - 1)
                rest = pl.ds(bases[g] + (1 - way) * n, n)
                xs2[d, way, rest, :] = bwd[d, rest, near].astype(BF)
                rows = pl.ds(bases[g] + way * n, n)
                s1copy(g, d, way).wait_recv()
                mine = bwd[d, rows, near] + xr1[d, way, pl.ds(bases[g] // 2, n), :].astype(F32)
                xs2[d, way, rows, :] = sealed(mine, n)
                s2copy(g, d, way).start()

    def rycopy(g, d):
        at = pl.ds(bases[g], counts[g])
        return remote(ysend.at[d, at], yrecv.at[d, at], rys.at[g, d], ryr.at[g, d], ydev(d))

    accs = [None, None]
    for g in (1, 0):
        at = pl.ds(bases[g], counts[g])
        for d in far_first:
            v = bwd[d, at, xlanes(0)]
            for way in (0, 1):
                s2copy(g, d, way).wait_recv()
                v = v + xr2[d, way, at, :].astype(F32)
            if d:
                ysend[d, at, :] = sealed(v, counts[g])
                rycopy(g, d).start()
            else:
                accs[g] = v

    def rzcopy(d):
        return remote(rsend.at[place_of(d)], rrecv.at[z], rzs.at[d], rzr.at[d], zdev(d))

    def send_back(v, base, first, end):
        shape = ((end - first) * 16, v.shape[0])
        r = iota(shape, 0)
        p = ((r >> 4) + first) * TOK + (r & 15) - base
        fit = (iota(shape, 1) == p) & ((r & 15) < TOK)
        placed = dot(jnp.where(fit, 1.0, 0.0).astype(BF), v).astype(BF)
        rsend[first:end] = placed.reshape(end - first, 16, LANE)
        for d in z_order[::-1]:
            if first <= place_of(d) < end:
                rzcopy(d).start()

    for g in (1, 0):
        at = pl.ds(bases[g], counts[g])
        for d in far_first[:NY - 1]:
            rycopy(g, d).wait_recv()
            accs[g] = accs[g] + yrecv[d, at, :].astype(F32)
        accs[g] = sealed(accs[g], counts[g])
        if g:
            send_back(accs[1], 64, 6, NZ)
    send_back(jnp.concatenate(accs, axis=0), 0, 0, 6)
    rrecv[z] = rsend[0]

    for d in z_order:
        rzcopy(d).wait_recv()
    out = jnp.zeros((TOK, LANE), F32)
    gout = [jnp.zeros((TOK, 1), F32) for _ in range(4)]
    for e in range(NZ // 2):
        hits = [chosen[k] == e for k in range(4)]
        w = jnp.zeros((TOK, 1), F32)
        for k in range(4):
            w = w + jnp.where(hits[k], weight[k], 0.0)
        v = rrecv[2 * e].astype(F32) + rrecv[2 * e + 1].astype(F32)
        v = v[0:TOK]
        out = out + w * v
        gate = v[:, FEAT:FEAT + 1] + v[:, FEAT + 1:FEAT + 2]
        gout = [gout[k] + jnp.where(hits[k], gate, 0.0) for k in range(4)]
    tg_out[...] = out[:, 0:FEAT].astype(BF)
    for k in range(4):
        gg_out[k:k + 1, :] = jnp.sum(jnp.where(small, gout[k], 0.0), axis=0, keepdims=True)

    for d in z_order:
        zcopy(d).wait_send()
        rzcopy(d).wait_send()
    wsend.wait_send()
    for cp in (psend, tswap, gswap):
        cp.wait_send()
    for d in range(NY):
        if d:
            for g in (0, 1):
                rycopy(g, d).wait_send()
                ycopy(g, d).wait_send()
        for way in (0, 1):
            for g in (0, 1):
                x1copy(g, d, way).wait_send()
                x2copy(g, d, way).wait_send()
                s1copy(g, d, way).wait_send()
                s2copy(g, d, way).wait_send()


def body(tokens, out_grad, expert_ids, gate_probs, w_gate, w_up, w_down):
    vmem = pl.BlockSpec(memory_space=pltpu.VMEM)
    hbm = pl.BlockSpec(memory_space=pltpu.HBM)
    dma = pltpu.SemaphoreType.DMA
    token_grad, gate_grad = pl.pallas_call(
        kernel,
        out_shape=(
            jax.ShapeDtypeStruct((TOK, FEAT), BF),
            jax.ShapeDtypeStruct((4, TOK), F32),
        ),
        in_specs=[hbm] * 7,
        out_specs=(vmem, vmem),
        scratch_shapes=[
            pltpu.VMEM((2, TOK, FEAT), BF),
            pltpu.VMEM((4, TOK), jnp.int32),
            pltpu.VMEM((4, TOK), F32),
            pltpu.VMEM((3, HID, SLICES * 2 * FEAT), BF),
            pltpu.VMEM((2, 3, HPAD, SLICES * LANE), BF),
            pltpu.VMEM((3, 2, HPAD, SLICES * LANE), BF),
            pltpu.VMEM((32, LANE), BF),
            pltpu.VMEM((NZ, 32, LANE), BF),
            pltpu.VMEM((SLICES, LANE, LANE), BF),
            pltpu.VMEM((SLICES, LANE, 2 * LANE), BF),
            pltpu.VMEM((3, 2, HPAD, 256), F32),
            pltpu.VMEM((3, HPAD, 256), F32),
            pltpu.VMEM((2, 2, HPAD, 256), BF),
            pltpu.VMEM((8, 256), F32),
            pltpu.VMEM((8, 256), F32),
            pltpu.VMEM((NY, ROWS, WIDE), F32),
            pltpu.VMEM((NY, 2, ROWS // 2, LANE), BF),
            pltpu.VMEM((NY, 2, ROWS // 2, LANE), BF),
            pltpu.VMEM((NY, 2, ROWS, LANE), BF),
            pltpu.VMEM((NY, 2, ROWS, LANE), BF),
            pltpu.VMEM((NY, ROWS, LANE), BF),
            pltpu.VMEM((NY, ROWS, LANE), BF),
            pltpu.VMEM((NZ, 16, LANE), BF),
            pltpu.VMEM((NZ, 16, LANE), BF),
            dma((4,)),
            dma((3,)),
            dma((1,)),
            dma((2,)),
            dma((6,)),
            dma((NZ,)), dma((NZ,)),
            dma((2, NY)), dma((2, NY)),
            dma((2, NY, 2)), dma((2, NY, 2)),
            dma((2, NY, 2)), dma((2, NY, 2)),
            dma((2, NY, 2)), dma((2, NY, 2)),
            dma((2, NY, 2)), dma((2, NY, 2)),
            dma((2, NY)), dma((2, NY)),
            dma((NZ,)), dma((NZ,)),
        ],
        compiler_params=pltpu.CompilerParams(
            collective_id=0, has_side_effects=True, vmem_limit_bytes=63 * 2**20
        ),
    )(tokens, out_grad, expert_ids.T, gate_probs.T, w_gate, w_up, w_down)
    return token_grad, gate_grad.T


def solution(mesh):
    in_specs = (
        P("expert", "tensor"),
        P("expert", "tensor"),
        P("expert", None),
        P("expert", None),
        P("expert", "tensor", None),
        P("expert", "tensor", None),
        P("expert", "tensor", None),
    )
    out_specs = (P("expert", "tensor"), P("expert", None))
    return jax.shard_map(body, mesh=mesh, in_specs=in_specs, out_specs=out_specs, check_vma=False)
```
